32 devices in a mesh: groups: 2 (over x), dp: 16 (over z, y, core).
Axes of the slice: x: 2, y: 2, z: 4, core: 2. Of those that a mesh axis runs over, the one named last changes fastest.
Arguments:
- queries: bfloat16 [4096, 2048], P(('groups', 'dp')), parts along dimension 0, may hold values from -6 to 6
- key_vectors: bfloat16 [4096, 512], P(('groups', 'dp')), parts along dimension 0, may hold values from -6 to 6
- value_vectors: bfloat16 [4096, 512], P(('groups', 'dp')), parts along dimension 0, may hold values from -6 to 6
- output_gradient: bfloat16 [4096, 2048], P(('groups', 'dp')), parts along dimension 0, may hold values from -6 to 6
- doc_lengths: int32 [16], P('groups'), parts along dimension 0, may hold values from 1 to 512, 2048 in all
Outputs:
- attention_result: bfloat16 [4096, 2048], P(('groups', 'dp')), parts along dimension 0
- query_gradient: bfloat16 [4096, 2048], P(('groups', 'dp')), parts along dimension 0
- grad_k: bfloat16 [4096, 512], P(('groups', 'dp')), parts along dimension 0
- grad_v: bfloat16 [4096, 512], P(('groups', 'dp')), parts along dimension 0
The draws below stay inside these ranges and needn't reach their ends.
There are 2 independent parts, one for each index of `groups`. The reference program is written for one: setup_inputs(seed, part) draws one part's arguments, and reference() takes and returns one part's arrays. A program takes and returns all parts, laid end to end along the dimension named above; each array names one. Nothing has to cross between parts.
Inputs may be any that keep to these rules, and one draw needn't show every extreme that they name: `doc_lengths`: the lengths sum to 2048; the longest document has exactly 512 tokens.
All inputs are finite; a program needn't handle non-finite values.
Results may differ from the reference program's by a relative error of at most 0.012.
Values may be sent and summed in bfloat16 or wider, within the bound.
A program may use at most 64 MiB of HBM per device.

```python
import math
import jax
import jax.numpy as jnp
import numpy as np
from jax import lax

HEAD_WIDTH = 128
QUERY_HEADS = 16
KEY_VALUE_HEADS = 4
TOK_DEV = 128
SPAN = 4
STREAM_TOKENS = 2048
DOCS = 8


def draw_queries(key, part):
    key = jax.random.fold_in(key, 3)
    outcome = jnp.clip(jax.random.normal(key, (STREAM_TOKENS, QUERY_HEADS * HEAD_WIDTH)), -6.0, 6.0)
    return outcome.astype(jnp.bfloat16)


def draw_key_vectors(key, part):
    key = jax.random.fold_in(key, 7)
    outcome = jnp.clip(jax.random.normal(key, (STREAM_TOKENS, KEY_VALUE_HEADS * HEAD_WIDTH)), -6.0, 6.0)
    return outcome.astype(jnp.bfloat16)


def level_of(own_key, shape, cuts, smallest, largest):
    def one(dim, parts):
        draws = jax.random.uniform(jax.random.fold_in(jax.random.fold_in(own_key, 6), dim), (parts,), jnp.float32, smallest / len(cuts), largest / len(cuts))
        return jnp.repeat(jnp.exp(draws), shape[dim] // parts).reshape((-1,) + (1,) * (len(shape) - dim - 1))

    gain = one(*cuts[0])
    for cut in cuts[1:]:
        gain = gain * one(*cut)
    return gain


def split_up(number_of, total, limit, skew):
    weights = [(1 << 20) // math.isqrt(standing ** skew) + 1 for standing in range(2, number_of + 1)]
    rest, holding = total - limit - (number_of - 1), [1] * (number_of - 1)
    while rest > 0:
        movable = [i for i in range(number_of - 1) if holding[i] < limit]
        whole, budget = sum([weights[i] for i in movable]), rest
        for i in movable:
            more = min(limit - holding[i], max(1, budget * weights[i] // whole), rest)
            holding[i] = holding[i] + more
            rest = rest - more
    return np.array([limit] + holding)


def uneven_parts(stream_key, amount, total, limit, slope):
    if amount == 2:
        one = jax.random.randint(stream_key, (), max(1, total - limit), min(limit, total - 1) + 1)
        return jnp.stack([one, total - one])
    sizes = jnp.asarray(split_up(amount, total, limit, slope), jnp.int32)
    pairs = (amount - 1) // 2
    giver, sink = sizes[1:1 + 2 * pairs:2], sizes[2:2 + 2 * pairs:2]
    room = jnp.minimum(giver - 1, limit - sink)
    passed = jax.random.randint(jax.random.fold_in(stream_key, 1), (pairs,), 0, 1 << 20) % (room + 1)
    sizes = sizes.at[1:1 + 2 * pairs:2].set(giver - passed).at[2:2 + 2 * pairs:2].set(sink + passed)
    return sizes[jax.random.permutation(jax.random.fold_in(stream_key, 2), amount)]


def centred(key, extent, width, most, cuts=(), held_as=jnp.bfloat16):
    entries = jax.random.normal(key, extent, jnp.float32) * width
    if len(cuts) > 0:
        entries = level_of(key, extent, cuts, -0.22, 0.18) * entries
    return jnp.clip(entries, min=-most, max=most).astype(held_as)


def setup_inputs(seed: int = 0, part: int = 0) -> dict:
    splits = jax.random.split(jax.random.key(seed), 6)
    part_keys = jax.random.split(jax.random.fold_in(splits[5], part), 6)
    return {
        "queries": draw_queries(jax.random.fold_in(jax.random.fold_in(splits[5], part), 71), part),
        "key_vectors": draw_key_vectors(jax.random.fold_in(jax.random.fold_in(splits[5], part), 71), part),
        "value_vectors": centred(part_keys[2], (STREAM_TOKENS, KEY_VALUE_HEADS * HEAD_WIDTH), 1.0, 6.0, ((0, 16),)),
        "output_gradient": centred(part_keys[3], (STREAM_TOKENS, QUERY_HEADS * HEAD_WIDTH), 1.0, 6.0, ((0, 16),)),
        "doc_lengths": uneven_parts(part_keys[4], DOCS, STREAM_TOKENS, SPAN * TOK_DEV, 2).astype(jnp.int32),
    }


masked_score = -1e+30

def segment_ids(doc_ends, positions):
    return lax.optimization_barrier(jnp.sum((doc_ends[None, :] <= positions[:, None]).astype(jnp.int32), axis=1)).astype(jnp.int32)

def rounded(array):
    return lax.optimization_barrier(array.astype(jnp.bfloat16)).astype(jnp.float32)

def score_grads(query_part, grad_part, log_sums, delta_rows, key_part, value_part, allowed, score_scale):
    scores = jnp.einsum('qhgd,khd->hgqk', query_part.astype(jnp.float32), key_part.astype(jnp.float32)) * score_scale
    log_t = jnp.transpose(log_sums, (1, 2, 0))[..., None]
    delta_t = jnp.transpose(delta_rows, (1, 2, 0))[..., None]
    probs = jnp.where(allowed[None, None], jnp.exp(scores - log_t), 0.0)
    prob_grads = jnp.einsum('qhgd,khd->hgqk', grad_part.astype(jnp.float32), value_part.astype(jnp.float32))
    return (rounded(probs * (prob_grads - delta_t)), rounded(probs))

def reference(queries, key_vectors, value_vectors, output_gradient, doc_lengths):
    group_width = QUERY_HEADS // KEY_VALUE_HEADS
    score_scale = 1.0 / math.sqrt(HEAD_WIDTH)
    block_rows = min(512, STREAM_TOKENS)
    window = min(STREAM_TOKENS, SPAN * TOK_DEV + block_rows)
    block_count = STREAM_TOKENS // block_rows
    doc_ends = jnp.cumsum(doc_lengths).astype(jnp.int32)
    positions = jnp.arange(STREAM_TOKENS, dtype=jnp.int32)
    segments = segment_ids(doc_ends, positions)
    query_tensor4 = queries.reshape(STREAM_TOKENS, KEY_VALUE_HEADS, group_width, HEAD_WIDTH)
    gradient4 = output_gradient.reshape(STREAM_TOKENS, KEY_VALUE_HEADS, group_width, HEAD_WIDTH)
    key_tensor3 = key_vectors.reshape(STREAM_TOKENS, KEY_VALUE_HEADS, HEAD_WIDTH)
    value_tensor3 = value_vectors.reshape(STREAM_TOKENS, KEY_VALUE_HEADS, HEAD_WIDTH)

    def take(array, start, length):
        return lax.dynamic_slice_in_dim(array, start.astype(jnp.int32), length, 0)

    def forward(block_index):
        q_start = (block_index * block_rows).astype(jnp.int32)
        k_start = jnp.clip(q_start - SPAN * TOK_DEV, 0, STREAM_TOKENS - window).astype(jnp.int32)
        q_pos = take(positions, q_start, block_rows)
        k_pos = take(positions, k_start, window)
        allowed = (k_pos[None, :] <= q_pos[:, None]) & (take(segments, k_start, window)[None, :] == take(segments, q_start, block_rows)[:, None])
        scores = jnp.einsum('qhgd,khd->hgqk', take(query_tensor4, q_start, block_rows).astype(jnp.float32), take(key_tensor3, k_start, window).astype(jnp.float32)) * score_scale
        scores = jnp.where(allowed[None, None], scores, masked_score)
        row_max = lax.optimization_barrier(jnp.max(scores, axis=-1, keepdims=True))
        weights = jnp.where(allowed[None, None], jnp.exp(scores - row_max), 0.0)
        weight_sum = lax.optimization_barrier(jnp.sum(weights, axis=-1, keepdims=True))
        mixed_rows = jnp.einsum('hgqk,khd->qhgd', rounded(weights), take(value_tensor3, k_start, window).astype(jnp.float32))
        mixed_rows = mixed_rows / jnp.transpose(weight_sum, (2, 0, 1, 3))
        log_sums = jnp.transpose(row_max + jnp.log(weight_sum), (2, 0, 1, 3))[..., 0]
        return (mixed_rows.astype(jnp.bfloat16), log_sums)
    mixed_all, logsum_total = lax.map(forward, jnp.arange(block_count, dtype=jnp.int32))
    attention_result = mixed_all.reshape(STREAM_TOKENS, QUERY_HEADS * HEAD_WIDTH)
    logsum_total = logsum_total.reshape(STREAM_TOKENS, KEY_VALUE_HEADS, group_width)
    delta_rows = lax.optimization_barrier(jnp.sum((output_gradient.astype(jnp.float32) * attention_result.astype(jnp.float32)).reshape(STREAM_TOKENS, KEY_VALUE_HEADS, group_width, HEAD_WIDTH), axis=-1))

    def query_side(block_index):
        q_start = (block_index * block_rows).astype(jnp.int32)
        k_start = jnp.clip(q_start - SPAN * TOK_DEV, 0, STREAM_TOKENS - window).astype(jnp.int32)
        q_pos = take(positions, q_start, block_rows)
        k_pos = take(positions, k_start, window)
        allowed = (k_pos[None, :] <= q_pos[:, None]) & (take(segments, k_start, window)[None, :] == take(segments, q_start, block_rows)[:, None])
        key_part = take(key_tensor3, k_start, window)
        score_grad, probs16 = score_grads(take(query_tensor4, q_start, block_rows), take(gradient4, q_start, block_rows), take(logsum_total, q_start, block_rows), take(delta_rows, q_start, block_rows), key_part, take(value_tensor3, k_start, window), allowed, score_scale)
        return (jnp.einsum('hgqk,khd->qhgd', score_grad, key_part.astype(jnp.float32)) * score_scale).astype(jnp.bfloat16)

    def key_side(block_index):
        k_start = (block_index * block_rows).astype(jnp.int32)
        q_start = jnp.clip(k_start, 0, STREAM_TOKENS - window).astype(jnp.int32)
        q_pos = take(positions, q_start, window)
        k_pos = take(positions, k_start, block_rows)
        allowed = (k_pos[None, :] <= q_pos[:, None]) & (take(segments, k_start, block_rows)[None, :] == take(segments, q_start, window)[:, None])
        query_part = take(query_tensor4, q_start, window)
        grad_part = take(gradient4, q_start, window)
        score_grad, probs16 = score_grads(query_part, grad_part, take(logsum_total, q_start, window), take(delta_rows, q_start, window), take(key_tensor3, k_start, block_rows), take(value_tensor3, k_start, block_rows), allowed, score_scale)
        key_grad = jnp.einsum('hgqk,qhgd->khd', score_grad, query_part.astype(jnp.float32)) * score_scale
        value_grad = jnp.einsum('hgqk,qhgd->khd', probs16, grad_part.astype(jnp.float32))
        return (key_grad.astype(jnp.bfloat16), value_grad.astype(jnp.bfloat16))
    query_gradient = lax.map(query_side, jnp.arange(block_count, dtype=jnp.int32)).reshape(STREAM_TOKENS, QUERY_HEADS * HEAD_WIDTH)
    key_gradients, value_gradients = lax.map(key_side, jnp.arange(block_count, dtype=jnp.int32))
    return (attention_result, query_gradient, key_gradients.reshape(STREAM_TOKENS, KEY_VALUE_HEADS * HEAD_WIDTH), value_gradients.reshape(STREAM_TOKENS, KEY_VALUE_HEADS * HEAD_WIDTH))
```

```python
import functools
import math

import jax
import jax.numpy as jnp
from jax import lax
from jax.experimental import pallas as pl
from jax.experimental.pallas import tpu as pltpu
from jax.sharding import PartitionSpec as P

HEAD_WIDTH = 128
QUERY_HEADS = 16
KEY_VALUE_HEADS = 4
SPAN = 4
GROUP = QUERY_HEADS // KEY_VALUE_HEADS
MESH = pl.DeviceIdType.MESH


def dims(lhs, rhs):
    return (((lhs,), (rhs,)), ((), ()))


def dot(a, b, lhs, rhs):
    return lax.dot_general(a, b, dims(lhs, rhs), preferred_element_type=jnp.float32)


def stacked(block):
    return jnp.concatenate(
        [block[:, j * HEAD_WIDTH : (j + 1) * HEAD_WIDTH] for j in range(GROUP)], axis=0
    )


def kernel(
    count,
    lens_ref,
    q_ref,
    k_ref,
    v_ref,
    g_ref,
    o_ref,
    dq_ref,
    dk_ref,
    dv_ref,
    win,
    part,
    got,
    own,
    bias,
    kv_send,
    kv_recv,
    part_send,
    part_recv,
):
    rows = q_ref.shape[0]
    group = lax.axis_index("groups")
    me = lax.axis_index("dp")
    scale = 1.0 / math.sqrt(HEAD_WIDTH)
    window = (SPAN + 1) * rows
    width = GROUP * HEAD_WIDTH

    barrier = pltpu.get_barrier_semaphore()
    for o in range(1, SPAN + 1):

        @pl.when(me >= o)
        def _():
            pl.semaphore_signal(barrier, inc=1, device_id=(group, me - o), device_id_type=MESH)

        @pl.when(me + o < count)
        def _():
            pl.semaphore_signal(barrier, inc=1, device_id=(group, me + o), device_id_type=MESH)

    for h in range(KEY_VALUE_HEADS):
        cols = slice(h * HEAD_WIDTH, (h + 1) * HEAD_WIDTH)
        win[h, 0, SPAN] = k_ref[:, cols]
        win[h, 1, SPAN] = v_ref[:, cols]

    pl.semaphore_wait(barrier, jnp.minimum(me, SPAN) + jnp.minimum(count - 1 - me, SPAN))

    def kv_copy(h, o):
        return pltpu.make_async_remote_copy(
            src_ref=win.at[h, :, SPAN],
            dst_ref=win.at[h, :, SPAN - o],
            send_sem=kv_send.at[h, o - 1],
            recv_sem=kv_recv.at[h, o - 1],
            device_id=(group, me + o),
            device_id_type=MESH,
        )

    def part_copy(h, o):
        return pltpu.make_async_remote_copy(
            src_ref=part.at[h, o - 1],
            dst_ref=got.at[h, o - 1],
            send_sem=part_send.at[h, o - 1],
            recv_sem=part_recv.at[h, o - 1],
            device_id=(group, me - o),
            device_id_type=MESH,
        )

    for h in range(KEY_VALUE_HEADS):
        for o in range(SPAN, 0, -1):

            @pl.when(me + o < count)
            def _():
                kv_copy(h, o).start()

    for o in range(1, SPAN + 1):

        @pl.when(me < o)
        def _():
            win[:, :, SPAN - o] = jnp.zeros_like(win[:, :, SPAN - o])

        @pl.when(me + o >= count)
        def _():
            got[:, o - 1] = jnp.zeros_like(got[:, o - 1])

    q_pos = me * rows + lax.broadcasted_iota(jnp.int32, (1, rows), 1)
    begin = jnp.zeros((1, rows), jnp.int32)
    doc_end = jnp.int32(0)
    for d in range(lens_ref.shape[0]):
        doc_end = doc_end + lens_ref[d]
        begin = jnp.where(q_pos >= doc_end, doc_end, begin)
    k_pos = (me - SPAN) * rows + lax.broadcasted_iota(jnp.int32, (window, rows), 0)
    bias[...] = jnp.where((k_pos >= begin) & (k_pos <= q_pos), 0.0, -1e30)

    def head(h, carry):
        for o in range(1, SPAN + 1):

            @pl.when(me >= o)
            def _():
                kv_copy(h, o).wait_recv()

        cols = pl.ds(pl.multiple_of(h * width, width), width)
        keys = win[h, 0].reshape(window, HEAD_WIDTH)
        values = win[h, 1].reshape(window, HEAD_WIDTH)
        q4 = stacked(q_ref[:, cols])
        g4 = stacked(g_ref[:, cols])
        scores = dot(keys, q4, 1, 1) + jnp.concatenate([bias[...]] * GROUP, axis=1)
        row_max = jnp.max(scores, axis=0, keepdims=True)
        weights = jnp.exp2((scores - row_max) * (scale / math.log(2.0)))
        inverse = 1.0 / jnp.sum(weights, axis=0, keepdims=True)
        mixed = dot(values, weights.astype(jnp.bfloat16), 0, 0) * inverse
        probs = weights * inverse
        prob_grads = dot(values, g4, 1, 1)
        terms = probs * prob_grads
        deltas = jnp.sum(terms, axis=0, keepdims=True)
        ds16 = (terms - probs * deltas).astype(jnp.bfloat16)
        p16 = probs.astype(jnp.bfloat16)
        dk = dot(ds16, q4, 1, 0) * scale
        dv = dot(p16, g4, 1, 0)
        for o in range(1, SPAN + 1):
            block = slice((SPAN - o) * rows, (SPAN - o + 1) * rows)
            part[h, o - 1, 0] = dk[block].astype(jnp.bfloat16)
            part[h, o - 1, 1] = dv[block].astype(jnp.bfloat16)
        own[h, 0] = dk[SPAN * rows :]
        own[h, 1] = dv[SPAN * rows :]
        for o in range(SPAN, 0, -1):

            @pl.when(me >= o)
            def _():
                part_copy(h, o).start()

        query_grad = dot(keys, ds16, 0, 0) * scale
        for j in range(GROUP):
            span = slice(j * rows, (j + 1) * rows)
            out = pl.ds(pl.multiple_of(h * width + j * HEAD_WIDTH, HEAD_WIDTH), HEAD_WIDTH)
            o_ref[:, out] = mixed[:, span].T.astype(jnp.bfloat16)
            dq_ref[:, out] = query_grad[:, span].T.astype(jnp.bfloat16)
        return carry

    lax.fori_loop(0, KEY_VALUE_HEADS, head, 0)

    def finish(h, carry):
        for o in range(1, SPAN + 1):

            @pl.when(me + o < count)
            def _():
                part_copy(h, o).wait_recv()
                kv_copy(h, o).wait_send()

            @pl.when(me >= o)
            def _():
                part_copy(h, o).wait_send()

        total = own[h]
        for o in range(1, SPAN + 1):
            total = total + got[h, o - 1].astype(jnp.float32)
        out = pl.ds(pl.multiple_of(h * HEAD_WIDTH, HEAD_WIDTH), HEAD_WIDTH)
        dk_ref[:, out] = total[0].astype(jnp.bfloat16)
        dv_ref[:, out] = total[1].astype(jnp.bfloat16)
        return carry

    lax.fori_loop(0, KEY_VALUE_HEADS, finish, 0)


def solution(mesh):
    count = mesh.shape["dp"]

    def body(queries, key_vectors, value_vectors, output_gradient, doc_lengths):
        rows = queries.shape[0]
        vmem = pl.BlockSpec(memory_space=pltpu.VMEM)
        pair = (2, rows, HEAD_WIDTH)
        heads = KEY_VALUE_HEADS
        return pl.pallas_call(
            functools.partial(kernel, count),
            out_shape=[
                jax.ShapeDtypeStruct(a.shape, jnp.bfloat16)
                for a in (queries, queries, key_vectors, value_vectors)
            ],
            in_specs=[pl.BlockSpec(memory_space=pltpu.SMEM)] + [vmem] * 4,
            out_specs=[vmem] * 4,
            scratch_shapes=[
                pltpu.VMEM((heads, 2, SPAN + 1, rows, HEAD_WIDTH), jnp.bfloat16),
                pltpu.VMEM((heads, SPAN) + pair, jnp.bfloat16),
                pltpu.VMEM((heads, SPAN) + pair, jnp.bfloat16),
                pltpu.VMEM((heads,) + pair, jnp.float32),
                pltpu.VMEM(((SPAN + 1) * rows, rows), jnp.float32),
            ]
            + [pltpu.SemaphoreType.DMA((heads, SPAN))] * 4,
            compiler_params=pltpu.CompilerParams(
                collective_id=0, has_side_effects=True, vmem_limit_bytes=48 * 1024 * 1024
            ),
            cost_estimate=pl.CostEstimate(
                flops=10 * rows * rows * (SPAN + 1) * QUERY_HEADS * HEAD_WIDTH,
                bytes_accessed=12 * rows * QUERY_HEADS * HEAD_WIDTH,
                transcendentals=rows * rows * (SPAN + 1) * QUERY_HEADS,
            ),
        )(doc_lengths, queries, key_vectors, value_vectors, output_gradient)

    spread = P(("groups", "dp"), None)
    return jax.shard_map(
        body,
        mesh=mesh,
        in_specs=(spread,) * 4 + (P("groups"),),
        out_specs=(spread,) * 4,
        check_vma=False,
    )
```

```python
import functools
import math

import jax
import jax.numpy as jnp
from jax import lax
from jax.experimental import pallas as pl
from jax.experimental.pallas import tpu as pltpu
from jax.sharding import PartitionSpec as P

HEAD_WIDTH = 128
QUERY_HEADS = 16
KEY_VALUE_HEADS = 4
SPAN = 4
GROUP = QUERY_HEADS // KEY_VALUE_HEADS
MESH = pl.DeviceIdType.MESH


def dims(lhs, rhs):
    return (((lhs,), (rhs,)), ((), ()))


def dot(a, b, lhs, rhs):
    return lax.dot_general(a, b, dims(lhs, rhs), preferred_element_type=jnp.float32)


def stacked(block):
    return jnp.concatenate(
        [block[:, j * HEAD_WIDTH : (j + 1) * HEAD_WIDTH] for j in range(GROUP)], axis=0
    )


def kernel(
    count,
    lens_ref,
    q_hbm,
    k_hbm,
    v_hbm,
    g_hbm,
    o_ref,
    dq_ref,
    dk_ref,
    dv_ref,
    q_ref,
    g_ref,
    win,
    mine,
    theirs,
    keep,
    out,
    got,
    own,
    bias,
    load_sem,
    kv_sem,
    far_send,
    sib_send,
    kv_recv,
    part_send,
    part_recv,
    out_send,
    out_recv,
):
    rows = q_ref.shape[0]
    group = lax.axis_index("groups")
    me = lax.axis_index("dp")
    core = lax.rem(me, 2)
    sibling = me + 1 - 2 * core
    scale = 1.0 / math.sqrt(HEAD_WIDTH)
    window = (SPAN + 1) * rows
    width = GROUP * HEAD_WIDTH
    far = (2, 4)

    def load_kv(h):
        cols = pl.ds(h * HEAD_WIDTH, HEAD_WIDTH)
        return [
            pltpu.make_async_copy(ref.at[:, cols], win.at[h, i, SPAN], kv_sem.at[h, i])
            for i, ref in enumerate((k_hbm, v_hbm))
        ]

    load_q = pltpu.make_async_copy(q_hbm, q_ref, load_sem.at[0])
    load_g = pltpu.make_async_copy(g_hbm, g_ref, load_sem.at[1])
    for h in range(KEY_VALUE_HEADS):
        for copy in load_kv(h):
            copy.start()
    load_q.start()
    load_g.start()

    barrier = pltpu.get_barrier_semaphore()
    pl.semaphore_signal(barrier, inc=1, device_id=(group, sibling), device_id_type=MESH)
    for o in far:

        @pl.when(me >= o)
        def _():
            pl.semaphore_signal(barrier, inc=1, device_id=(group, me - o), device_id_type=MESH)

        @pl.when(me + o < count)
        def _():
            pl.semaphore_signal(barrier, inc=1, device_id=(group, me + o), device_id_type=MESH)

    for o in range(1, SPAN + 1):

        @pl.when(me < o)
        def _():
            win[:, :, SPAN - o] = jnp.zeros_like(win[:, :, SPAN - o])

    for i, o in enumerate(far):

        @pl.when(me + o >= count)
        def _():
            got[:, i] = jnp.zeros_like(got[:, i])

    q_pos = me * rows + lax.broadcasted_iota(jnp.int32, (1, rows), 1)
    begin = jnp.zeros((1, rows), jnp.int32)
    doc_end = jnp.int32(0)
    for d in range(lens_ref.shape[0]):
        doc_end = doc_end + lens_ref[d]
        begin = jnp.where(q_pos >= doc_end, doc_end, begin)
    k_pos = (me - SPAN) * rows + lax.broadcasted_iota(jnp.int32, (window, rows), 0)
    bias[...] = jnp.where((k_pos >= begin) & (k_pos <= q_pos), 0.0, -1e30)

    partners = jnp.int32(1)
    for o in far:
        partners = partners + jnp.where(me >= o, 1, 0) + jnp.where(me + o < count, 1, 0)
    pl.semaphore_wait(barrier, partners)

    def far_copy(h, i):
        return pltpu.make_async_remote_copy(
            src_ref=win.at[h, :, SPAN],
            dst_ref=win.at[h, :, SPAN - far[i]],
            send_sem=far_send.at[h, i],
            recv_sem=kv_recv.at[h, SPAN - far[i]],
            device_id=(group, me + far[i]),
            device_id_type=MESH,
        )

    def sib_copy(h, slot):
        return pltpu.make_async_remote_copy(
            src_ref=win.at[h, :, slot + 1 - 2 * core],
            dst_ref=win.at[h, :, slot],
            send_sem=sib_send.at[h, slot // 2],
            recv_sem=kv_recv.at[h, slot],
            device_id=(group, sibling),
            device_id_type=MESH,
        )

    def part_copy(h):
        return pltpu.make_async_remote_copy(
            src_ref=mine.at[h],
            dst_ref=theirs.at[h],
            send_sem=part_send.at[h],
            recv_sem=part_recv.at[h],
            device_id=(group, sibling),
            device_id_type=MESH,
        )

    def out_copy(h, i):
        return pltpu.make_async_remote_copy(
            src_ref=out.at[h, i],
            dst_ref=got.at[h, i],
            send_sem=out_send.at[h, i],
            recv_sem=out_recv.at[h, i],
            device_id=(group, me - far[i]),
            device_id_type=MESH,
        )

    for h in range(KEY_VALUE_HEADS):
        for copy in load_kv(h):
            copy.wait()
        for i in (1, 0):

            @pl.when(me + far[i] < count)
            def _():
                far_copy(h, i).start()

        @pl.when(core == 0)
        def _():
            sib_copy(h, 3).start()

    def forward(h):
        @pl.when(me >= 2)
        def _():
            far_copy(h, 0).wait_recv()

        @pl.when((me >= 2) & (core == 1))
        def _():
            sib_copy(h, 3).start()

        @pl.when(me >= 4)
        def _():
            far_copy(h, 1).wait_recv()

        @pl.when(me >= 2 + 2 * core)
        def _():
            sib_copy(h, 1).start()

    def pass_on(h):
        part_copy(h).wait_recv()
        near = keep[h, 0] + theirs[h, 1 - core].astype(jnp.float32)
        out[h, 0] = near.astype(jnp.bfloat16)
        extra = jnp.where(core == 1, theirs[h, 1].astype(jnp.float32), 0.0)
        out[h, 1] = (keep[h, 1] + extra).astype(jnp.bfloat16)
        for i in (1, 0):

            @pl.when(me >= far[i])
            def _():
                out_copy(h, i).start()

    forward(0)
    load_q.wait()
    load_g.wait()

    def head(h, carry):
        for slot in (3, 1):

            @pl.when(me >= SPAN - slot)
            def _():
                sib_copy(h, slot).wait_recv()

        cols = pl.ds(pl.multiple_of(h * width, width), width)
        keys = win[h, 0].reshape(window, HEAD_WIDTH)
        values = win[h, 1].reshape(window, HEAD_WIDTH)
        q4 = stacked(q_ref[:, cols])
        g4 = stacked(g_ref[:, cols])
        scores = dot(keys, q4, 1, 1) + jnp.concatenate([bias[...]] * GROUP, axis=1)
        row_max = jnp.max(scores, axis=0, keepdims=True)
        weights = jnp.exp2((scores - row_max) * (scale / math.log(2.0)))
        inverse = 1.0 / jnp.sum(weights, axis=0, keepdims=True)
        mixed = dot(values, weights.astype(jnp.bfloat16), 0, 0) * inverse

        @pl.when(h + 1 < KEY_VALUE_HEADS)
        def _():
            forward(h + 1)

        probs = weights * inverse
        prob_grads = dot(values, g4, 1, 1)
        terms = probs * prob_grads
        deltas = jnp.sum(terms, axis=0, keepdims=True)
        ds16 = (terms - probs * deltas).astype(jnp.bfloat16)
        p16 = probs.astype(jnp.bfloat16)
        dk = dot(ds16, q4, 1, 0) * scale
        dv = dot(p16, g4, 1, 0)
        for i, grad in enumerate((dk, dv)):
            blocks = [grad[b * rows : (b + 1) * rows] for b in range(SPAN + 1)]
            mine[h, 0, i] = blocks[3].astype(jnp.bfloat16)
            mine[h, 1, i] = blocks[1].astype(jnp.bfloat16)
            keep[h, 0, i] = blocks[2]
            keep[h, 1, i] = blocks[0]
            own[h, i] = blocks[4]
        part_copy(h).start()

        query_grad = dot(keys, ds16, 0, 0) * scale
        for j in range(GROUP):
            span = slice(j * rows, (j + 1) * rows)
            part = pl.ds(pl.multiple_of(h * width + j * HEAD_WIDTH, HEAD_WIDTH), HEAD_WIDTH)
            o_ref[:, part] = mixed[:, span].T.astype(jnp.bfloat16)
            dq_ref[:, part] = query_grad[:, span].T.astype(jnp.bfloat16)

        pass_on(h)
        return carry

    lax.fori_loop(0, KEY_VALUE_HEADS, head, 0)

    def finish(h, carry):
        for i in (0, 1):

            @pl.when(me + far[i] < count)
            def _():
                far_copy(h, i).wait_send()
                out_copy(h, i).wait_recv()

            @pl.when(me >= far[i])
            def _():
                out_copy(h, i).wait_send()

        @pl.when(me >= 2 * core)
        def _():
            sib_copy(h, 3).wait_send()

        @pl.when(me >= 2 + 2 * core)
        def _():
            sib_copy(h, 1).wait_send()

        part_copy(h).wait_send()
        total = own[h] + jnp.where(core == 0, theirs[h, 0].astype(jnp.float32), 0.0)
        for i in (0, 1):
            total = total + got[h, i].astype(jnp.float32)
        part = pl.ds(pl.multiple_of(h * HEAD_WIDTH, HEAD_WIDTH), HEAD_WIDTH)
        dk_ref[:, part] = total[0].astype(jnp.bfloat16)
        dv_ref[:, part] = total[1].astype(jnp.bfloat16)
        return carry

    lax.fori_loop(0, KEY_VALUE_HEADS, finish, 0)


def solution(mesh):
    count = mesh.shape["dp"]

    def body(queries, key_vectors, value_vectors, output_gradient, doc_lengths):
        rows = queries.shape[0]
        vmem = pl.BlockSpec(memory_space=pltpu.VMEM)
        pair = (2, rows, HEAD_WIDTH)
        heads = KEY_VALUE_HEADS
        return pl.pallas_call(
            functools.partial(kernel, count),
            out_shape=[
                jax.ShapeDtypeStruct(a.shape, jnp.bfloat16)
                for a in (queries, queries, key_vectors, value_vectors)
            ],
            in_specs=[pl.BlockSpec(memory_space=pltpu.SMEM)]
            + [pl.BlockSpec(memory_space=pltpu.HBM)] * 4,
            out_specs=[vmem] * 4,
            scratch_shapes=[
                pltpu.VMEM(queries.shape, jnp.bfloat16),
                pltpu.VMEM(queries.shape, jnp.bfloat16),
                pltpu.VMEM((heads, 2, SPAN + 1, rows, HEAD_WIDTH), jnp.bfloat16),
                pltpu.VMEM((heads, 2) + pair, jnp.bfloat16),
                pltpu.VMEM((heads, 2) + pair, jnp.bfloat16),
                pltpu.VMEM((heads, 2) + pair, jnp.float32),
                pltpu.VMEM((heads, 2) + pair, jnp.bfloat16),
                pltpu.VMEM((heads, 2) + pair, jnp.bfloat16),
                pltpu.VMEM((heads,) + pair, jnp.float32),
                pltpu.VMEM(((SPAN + 1) * rows, rows), jnp.float32),
                pltpu.SemaphoreType.DMA((2,)),
                pltpu.SemaphoreType.DMA((heads, 2)),
                pltpu.SemaphoreType.DMA((heads, 2)),
                pltpu.SemaphoreType.DMA((heads, 2)),
                pltpu.SemaphoreType.DMA((heads, SPAN)),
                pltpu.SemaphoreType.DMA((heads,)),
                pltpu.SemaphoreType.DMA((heads,)),
                pltpu.SemaphoreType.DMA((heads, 2)),
                pltpu.SemaphoreType.DMA((heads, 2)),
            ],
            compiler_params=pltpu.CompilerParams(
                collective_id=0, has_side_effects=True, vmem_limit_bytes=48 * 1024 * 1024
            ),
            cost_estimate=pl.CostEstimate(
                flops=10 * rows * rows * (SPAN + 1) * QUERY_HEADS * HEAD_WIDTH,
                bytes_accessed=12 * rows * QUERY_HEADS * HEAD_WIDTH,
                transcendentals=rows * rows * (SPAN + 1) * QUERY_HEADS,
            ),
        )(doc_lengths, queries, key_vectors, value_vectors, output_gradient)

    spread = P(("groups", "dp"), None)
    return jax.shard_map(
        body,
        mesh=mesh,
        in_specs=(spread,) * 4 + (P("groups"),),
        out_specs=(spread,) * 4,
        check_vma=False,
    )
```

```python
import functools
import math

import jax
import jax.numpy as jnp
from jax import lax
from jax.experimental import pallas as pl
from jax.experimental.pallas import tpu as pltpu
from jax.sharding import PartitionSpec as P

HEAD_WIDTH = 128
QUERY_HEADS = 16
KEY_VALUE_HEADS = 4
SPAN = 4
GROUP = QUERY_HEADS // KEY_VALUE_HEADS
MESH = pl.DeviceIdType.MESH


def dims(lhs, rhs):
    return (((lhs,), (rhs,)), ((), ()))


def dot(a, b, lhs, rhs):
    return lax.dot_general(a, b, dims(lhs, rhs), preferred_element_type=jnp.float32)


def stacked(block):
    return jnp.concatenate(
        [block[:, j * HEAD_WIDTH : (j + 1) * HEAD_WIDTH] for j in range(GROUP)], axis=0
    )


def kernel(
    count,
    lens_ref,
    q_hbm,
    k_hbm,
    v_hbm,
    g_hbm,
    o_hbm,
    dq_hbm,
    dk_hbm,
    dv_hbm,
    o_ref,
    dq_ref,
    dk_ref,
    dv_ref,
    q_ref,
    g_ref,
    win,
    mine,
    theirs,
    keep,
    out,
    got,
    own,
    bias,
    load_sem,
    kv_sem,
    far_send,
    sib_send,
    kv_recv,
    part_send,
    part_recv,
    out_send,
    out_recv,
    store_sem,
):
    rows = q_ref.shape[0]
    group = lax.axis_index("groups")
    me = lax.axis_index("dp")
    core = lax.rem(me, 2)
    sibling = me + 1 - 2 * core
    scale = 1.0 / math.sqrt(HEAD_WIDTH)
    window = (SPAN + 1) * rows
    width = GROUP * HEAD_WIDTH
    far = (2, 4)

    def load_kv(h):
        cols = pl.ds(h * HEAD_WIDTH, HEAD_WIDTH)
        return [
            pltpu.make_async_copy(ref.at[:, cols], win.at[h, i, SPAN], kv_sem.at[h, i])
            for i, ref in enumerate((k_hbm, v_hbm))
        ]

    load_q = pltpu.make_async_copy(q_hbm, q_ref, load_sem.at[0])
    load_g = pltpu.make_async_copy(g_hbm, g_ref, load_sem.at[1])
    for h in range(KEY_VALUE_HEADS):
        for copy in load_kv(h):
            copy.start()
    load_q.start()
    load_g.start()

    barrier = pltpu.get_barrier_semaphore()
    pl.semaphore_signal(barrier, inc=1, device_id=(group, sibling), device_id_type=MESH)
    for o in far:

        @pl.when(me >= o)
        def _():
            pl.semaphore_signal(barrier, inc=1, device_id=(group, me - o), device_id_type=MESH)

        @pl.when(me + o < count)
        def _():
            pl.semaphore_signal(barrier, inc=1, device_id=(group, me + o), device_id_type=MESH)

    for o in range(1, SPAN + 1):

        @pl.when(me < o)
        def _():
            win[:, :, SPAN - o] = jnp.zeros_like(win[:, :, SPAN - o])

    for i, o in enumerate(far):

        @pl.when(me + o >= count)
        def _():
            got[:, i] = jnp.zeros_like(got[:, i])

    q_pos = me * rows + lax.broadcasted_iota(jnp.int32, (1, rows), 1)
    begin = jnp.zeros((1, rows), jnp.int32)
    doc_end = jnp.int32(0)
    for d in range(lens_ref.shape[0]):
        doc_end = doc_end + lens_ref[d]
        begin = jnp.where(q_pos >= doc_end, doc_end, begin)
    k_pos = (me - SPAN) * rows + lax.broadcasted_iota(jnp.int32, (window, rows), 0)
    bias[...] = jnp.where((k_pos >= begin) & (k_pos <= q_pos), 0.0, -1e30)

    partners = jnp.int32(1)
    for o in far:
        partners = partners + jnp.where(me >= o, 1, 0) + jnp.where(me + o < count, 1, 0)
    pl.semaphore_wait(barrier, partners)

    def far_copy(h, i):
        return pltpu.make_async_remote_copy(
            src_ref=win.at[h, :, SPAN],
            dst_ref=win.at[h, :, SPAN - far[i]],
            send_sem=far_send.at[h, i],
            recv_sem=kv_recv.at[h, SPAN - far[i]],
            device_id=(group, me + far[i]),
            device_id_type=MESH,
        )

    def sib_copy(h, slot):
        return pltpu.make_async_remote_copy(
            src_ref=win.at[h, :, slot + 1 - 2 * core],
            dst_ref=win.at[h, :, slot],
            send_sem=sib_send.at[h, slot // 2],
            recv_sem=kv_recv.at[h, slot],
            device_id=(group, sibling),
            device_id_type=MESH,
        )

    def part_copy(h):
        return pltpu.make_async_remote_copy(
            src_ref=mine.at[h],
            dst_ref=theirs.at[h],
            send_sem=part_send.at[h],
            recv_sem=part_recv.at[h],
            device_id=(group, sibling),
            device_id_type=MESH,
        )

    def out_copy(h, i):
        return pltpu.make_async_remote_copy(
            src_ref=out.at[h, i],
            dst_ref=got.at[h, i],
            send_sem=out_send.at[h, i],
            recv_sem=out_recv.at[h, i],
            device_id=(group, me - far[i]),
            device_id_type=MESH,
        )

    for h in range(KEY_VALUE_HEADS):
        for copy in load_kv(h):
            copy.wait()
        for i in (1, 0):

            @pl.when(me + far[i] < count)
            def _():
                far_copy(h, i).start()

        @pl.when(core == 0)
        def _():
            sib_copy(h, 3).start()

    def forward(h):
        @pl.when(me >= 2)
        def _():
            far_copy(h, 0).wait_recv()

        @pl.when((me >= 2) & (core == 1))
        def _():
            sib_copy(h, 3).start()

        @pl.when(me >= 4)
        def _():
            far_copy(h, 1).wait_recv()

        @pl.when(me >= 2 + 2 * core)
        def _():
            sib_copy(h, 1).start()

    def pass_on(h):
        part_copy(h).wait_recv()
        near = keep[h, 0] + theirs[h, 1 - core].astype(jnp.float32)
        out[h, 0] = near.astype(jnp.bfloat16)
        extra = jnp.where(core == 1, theirs[h, 1].astype(jnp.float32), 0.0)
        out[h, 1] = (keep[h, 1] + extra).astype(jnp.bfloat16)
        for i in (1, 0):

            @pl.when(me >= far[i])
            def _():
                out_copy(h, i).start()

    def store(h):
        cols = pl.ds(pl.multiple_of(h * width, width), width)
        return [
            pltpu.make_async_copy(o_ref.at[:, cols], o_hbm.at[:, cols], store_sem.at[h, 0]),
            pltpu.make_async_copy(dq_ref.at[:, cols], dq_hbm.at[:, cols], store_sem.at[h, 1]),
        ]

    def store_grads(h):
        cols = pl.ds(pl.multiple_of(h * HEAD_WIDTH, HEAD_WIDTH), HEAD_WIDTH)
        return [
            pltpu.make_async_copy(dk_ref.at[:, cols], dk_hbm.at[:, cols], store_sem.at[h, 2]),
            pltpu.make_async_copy(dv_ref.at[:, cols], dv_hbm.at[:, cols], store_sem.at[h, 3]),
        ]

    forward(0)
    load_q.wait()
    load_g.wait()

    def head(h, carry):
        for slot in (3, 1):

            @pl.when(me >= SPAN - slot)
            def _():
                sib_copy(h, slot).wait_recv()

        cols = pl.ds(pl.multiple_of(h * width, width), width)
        keys = win[h, 0].reshape(window, HEAD_WIDTH)
        values = win[h, 1].reshape(window, HEAD_WIDTH)
        q4 = stacked(q_ref[:, cols])
        g4 = stacked(g_ref[:, cols])
        scores = dot(keys, q4, 1, 1) + jnp.concatenate([bias[...]] * GROUP, axis=1)
        row_max = jnp.max(scores, axis=0, keepdims=True)
        weights = jnp.exp2((scores - row_max) * (scale / math.log(2.0)))
        inverse = 1.0 / jnp.sum(weights, axis=0, keepdims=True)
        mixed = dot(values, weights.astype(jnp.bfloat16), 0, 0) * inverse

        @pl.when(h + 1 < KEY_VALUE_HEADS)
        def _():
            forward(h + 1)

        @pl.when(h >= 1)
        def _():
            pass_on(h - 1)

        probs = weights * inverse
        prob_grads = dot(values, g4, 1, 1)
        terms = probs * prob_grads
        deltas = jnp.sum(terms, axis=0, keepdims=True)
        ds16 = (terms - probs * deltas).astype(jnp.bfloat16)
        p16 = probs.astype(jnp.bfloat16)
        dk = dot(ds16, q4, 1, 0) * scale
        dv = dot(p16, g4, 1, 0)
        for i, grad in enumerate((dk, dv)):
            blocks = [grad[b * rows : (b + 1) * rows] for b in range(SPAN + 1)]
            mine[h, 0, i] = blocks[3].astype(jnp.bfloat16)
            mine[h, 1, i] = blocks[1].astype(jnp.bfloat16)
            keep[h, 0, i] = blocks[2]
            keep[h, 1, i] = blocks[0]
            own[h, i] = blocks[4]
        part_copy(h).start()

        query_grad = dot(keys, ds16, 0, 0) * scale
        for j in range(GROUP):
            span = slice(j * rows, (j + 1) * rows)
            part = pl.ds(pl.multiple_of(h * width + j * HEAD_WIDTH, HEAD_WIDTH), HEAD_WIDTH)
            o_ref[:, part] = mixed[:, span].T.astype(jnp.bfloat16)
            dq_ref[:, part] = query_grad[:, span].T.astype(jnp.bfloat16)

        for copy in store(h):
            copy.start()
        return carry

    lax.fori_loop(0, KEY_VALUE_HEADS, head, 0)
    pass_on(KEY_VALUE_HEADS - 1)

    def finish(h, carry):
        for i in (0, 1):

            @pl.when(me + far[i] < count)
            def _():
                far_copy(h, i).wait_send()
                out_copy(h, i).wait_recv()

            @pl.when(me >= far[i])
            def _():
                out_copy(h, i).wait_send()

        @pl.when(me >= 2 * core)
        def _():
            sib_copy(h, 3).wait_send()

        @pl.when(me >= 2 + 2 * core)
        def _():
            sib_copy(h, 1).wait_send()

        part_copy(h).wait_send()
        total = own[h] + jnp.where(core == 0, theirs[h, 0].astype(jnp.float32), 0.0)
        for i in (0, 1):
            total = total + got[h, i].astype(jnp.float32)
        part = pl.ds(pl.multiple_of(h * HEAD_WIDTH, HEAD_WIDTH), HEAD_WIDTH)
        dk_ref[:, part] = total[0].astype(jnp.bfloat16)
        dv_ref[:, part] = total[1].astype(jnp.bfloat16)
        for copy in store_grads(h):
            copy.start()
        return carry

    lax.fori_loop(0, KEY_VALUE_HEADS, finish, 0)
    for h in range(KEY_VALUE_HEADS):
        for copy in store(h) + store_grads(h):
            copy.wait()


def place(*refs):
    sources, results, held, load_sem, store_sem = refs[:4], refs[4:8], refs[8:12], refs[12], refs[13]
    loads = [
        pltpu.make_async_copy(source, block, load_sem.at[i])
        for i, (source, block) in enumerate(zip(sources, held))
    ]
    stores = [
        pltpu.make_async_copy(block, result, store_sem.at[i])
        for i, (block, result) in enumerate(zip(held, results))
    ]
    for load in loads:
        load.start()
    for load, store in zip(loads, stores):
        load.wait()
        store.start()
    for store in stores:
        store.wait()


def solution(mesh):
    count = mesh.shape["dp"]

    def body(queries, key_vectors, value_vectors, output_gradient, doc_lengths):
        rows = queries.shape[0]
        hbm = pl.BlockSpec(memory_space=pl.ANY)
        pair = (2, rows, HEAD_WIDTH)
        heads = KEY_VALUE_HEADS
        arrays = (queries, queries, key_vectors, value_vectors)
        shapes = [jax.ShapeDtypeStruct(a.shape, jnp.bfloat16) for a in arrays]
        results = pl.pallas_call(
            functools.partial(kernel, count),
            out_shape=shapes,
            in_specs=[pl.BlockSpec(memory_space=pltpu.SMEM)] + [hbm] * 4,
            out_specs=[hbm] * 4,
            scratch_shapes=[pltpu.VMEM(a.shape, jnp.bfloat16) for a in arrays]
            + [
                pltpu.VMEM(queries.shape, jnp.bfloat16),
                pltpu.VMEM(queries.shape, jnp.bfloat16),
                pltpu.VMEM((heads, 2, SPAN + 1, rows, HEAD_WIDTH), jnp.bfloat16),
                pltpu.VMEM((heads, 2) + pair, jnp.bfloat16),
                pltpu.VMEM((heads, 2) + pair, jnp.bfloat16),
                pltpu.VMEM((heads, 2) + pair, jnp.float32),
                pltpu.VMEM((heads, 2) + pair, jnp.bfloat16),
                pltpu.VMEM((heads, 2) + pair, jnp.bfloat16),
                pltpu.VMEM((heads,) + pair, jnp.float32),
                pltpu.VMEM(((SPAN + 1) * rows, rows), jnp.float32),
                pltpu.SemaphoreType.DMA((2,)),
                pltpu.SemaphoreType.DMA((heads, 2)),
                pltpu.SemaphoreType.DMA((heads, 2)),
                pltpu.SemaphoreType.DMA((heads, 2)),
                pltpu.SemaphoreType.DMA((heads, SPAN)),
                pltpu.SemaphoreType.DMA((heads,)),
                pltpu.SemaphoreType.DMA((heads,)),
                pltpu.SemaphoreType.DMA((heads, 2)),
                pltpu.SemaphoreType.DMA((heads, 2)),
                pltpu.SemaphoreType.DMA((heads, 4)),
            ],
            compiler_params=pltpu.CompilerParams(
                collective_id=0, has_side_effects=True, vmem_limit_bytes=63 * 1024 * 1024
            ),
            cost_estimate=pl.CostEstimate(
                flops=10 * rows * rows * (SPAN + 1) * QUERY_HEADS * HEAD_WIDTH,
                bytes_accessed=12 * rows * QUERY_HEADS * HEAD_WIDTH,
                transcendentals=rows * rows * (SPAN + 1) * QUERY_HEADS,
            ),
        )(doc_lengths, queries, key_vectors, value_vectors, output_gradient)
        return pl.pallas_call(
            place,
            out_shape=shapes,
            in_specs=[hbm] * 4,
            out_specs=[hbm] * 4,
            scratch_shapes=[pltpu.VMEM(a.shape, jnp.bfloat16) for a in arrays]
            + [pltpu.SemaphoreType.DMA((4,))] * 2,
            compiler_params=pltpu.CompilerParams(vmem_limit_bytes=63 * 1024 * 1024),
        )(*results)

    spread = P(("groups", "dp"), None)
    return jax.shard_map(
        body,
        mesh=mesh,
        in_specs=(spread,) * 4 + (P("groups"),),
        out_specs=(spread,) * 4,
        check_vma=False,
    )
```

```python
import functools
import math

import jax
import jax.numpy as jnp
from jax import lax
from jax.experimental import pallas as pl
from jax.experimental.pallas import tpu as pltpu
from jax.sharding import PartitionSpec as P

HEAD_WIDTH = 128
QUERY_HEADS = 16
KEY_VALUE_HEADS = 4
SPAN = 4
GROUP = QUERY_HEADS // KEY_VALUE_HEADS
MESH = pl.DeviceIdType.MESH


def dims(lhs, rhs):
    return (((lhs,), (rhs,)), ((), ()))


def dot(a, b, lhs, rhs):
    return lax.dot_general(a, b, dims(lhs, rhs), preferred_element_type=jnp.float32)


def stacked(block):
    return jnp.concatenate(
        [block[:, j * HEAD_WIDTH : (j + 1) * HEAD_WIDTH] for j in range(GROUP)], axis=0
    )


def kernel(
    count,
    lens_ref,
    q_hbm,
    k_hbm,
    v_hbm,
    g_hbm,
    o_hbm,
    dq_hbm,
    dk_hbm,
    dv_hbm,
    o_ref,
    dq_ref,
    dk_ref,
    dv_ref,
    q_ref,
    g_ref,
    win,
    mine,
    theirs,
    keep,
    out,
    got,
    own,
    bias,
    load_sem,
    kv_sem,
    far_send,
    sib_send,
    kv_recv,
    part_send,
    part_recv,
    out_send,
    out_recv,
    store_sem,
):
    rows = q_ref.shape[0]
    group = lax.axis_index("groups")
    me = lax.axis_index("dp")
    core = lax.rem(me, 2)
    sibling = me + 1 - 2 * core
    scale = 1.0 / math.sqrt(HEAD_WIDTH)
    window = (SPAN + 1) * rows
    width = GROUP * HEAD_WIDTH
    far = (2, 4)

    def load_kv(h):
        cols = pl.ds(h * HEAD_WIDTH, HEAD_WIDTH)
        return [
            pltpu.make_async_copy(ref.at[:, cols], win.at[h, i, SPAN], kv_sem.at[h, i])
            for i, ref in enumerate((k_hbm, v_hbm))
        ]

    load_q = pltpu.make_async_copy(q_hbm, q_ref, load_sem.at[0])
    load_g = pltpu.make_async_copy(g_hbm, g_ref, load_sem.at[1])
    for h in range(KEY_VALUE_HEADS):
        for copy in load_kv(h):
            copy.start()
    load_q.start()
    load_g.start()

    barrier = pltpu.get_barrier_semaphore()
    pl.semaphore_signal(barrier, inc=1, device_id=(group, sibling), device_id_type=MESH)
    for o in far:

        @pl.when(me >= o)
        def _():
            pl.semaphore_signal(barrier, inc=1, device_id=(group, me - o), device_id_type=MESH)

        @pl.when(me + o < count)
        def _():
            pl.semaphore_signal(barrier, inc=1, device_id=(group, me + o), device_id_type=MESH)

    for o in range(1, SPAN + 1):

        @pl.when(me < o)
        def _():
            win[:, :, SPAN - o] = jnp.zeros_like(win[:, :, SPAN - o])

    for i, o in enumerate(far):

        @pl.when(me + o >= count)
        def _():
            got[:, i] = jnp.zeros_like(got[:, i])

    q_pos = me * rows + lax.broadcasted_iota(jnp.int32, (1, rows), 1)
    begin = jnp.zeros((1, rows), jnp.int32)
    doc_end = jnp.int32(0)
    for d in range(lens_ref.shape[0]):
        doc_end = doc_end + lens_ref[d]
        begin = jnp.where(q_pos >= doc_end, doc_end, begin)
    k_pos = (me - SPAN) * rows + lax.broadcasted_iota(jnp.int32, (window, rows), 0)
    bias[...] = jnp.where((k_pos >= begin) & (k_pos <= q_pos), 0.0, -1e30)

    partners = jnp.int32(1)
    for o in far:
        partners = partners + jnp.where(me >= o, 1, 0) + jnp.where(me + o < count, 1, 0)
    pl.semaphore_wait(barrier, partners)

    def far_copy(h, i):
        return pltpu.make_async_remote_copy(
            src_ref=win.at[h, :, SPAN],
            dst_ref=win.at[h, :, SPAN - far[i]],
            send_sem=far_send.at[h, i],
            recv_sem=kv_recv.at[h, SPAN - far[i]],
            device_id=(group, me + far[i]),
            device_id_type=MESH,
        )

    def sib_copy(h, slot):
        return pltpu.make_async_remote_copy(
            src_ref=win.at[h, :, slot + 1 - 2 * core],
            dst_ref=win.at[h, :, slot],
            send_sem=sib_send.at[h, slot // 2],
            recv_sem=kv_recv.at[h, slot],
            device_id=(group, sibling),
            device_id_type=MESH,
        )

    def part_copy(h):
        return pltpu.make_async_remote_copy(
            src_ref=mine.at[h],
            dst_ref=theirs.at[h],
            send_sem=part_send.at[h],
            recv_sem=part_recv.at[h],
            device_id=(group, sibling),
            device_id_type=MESH,
        )

    def out_copy(h, i):
        return pltpu.make_async_remote_copy(
            src_ref=out.at[h, i],
            dst_ref=got.at[h, i],
            send_sem=out_send.at[h, i],
            recv_sem=out_recv.at[h, i],
            device_id=(group, me - far[i]),
            device_id_type=MESH,
        )

    def send_far(h):
        for i in (0, 1):

            @pl.when(me + far[i] < count)
            def _():
                far_copy(h, i).start()

    for h in range(KEY_VALUE_HEADS):
        for copy in load_kv(h):
            copy.wait()
        if h < 2:
            send_far(h)

        @pl.when(core == 0)
        def _():
            sib_copy(h, 3).start()

    def forward(h):
        @pl.when(me >= 2)
        def _():
            far_copy(h, 0).wait_recv()

        @pl.when((me >= 2) & (core == 1))
        def _():
            sib_copy(h, 3).start()

        @pl.when(me >= 4)
        def _():
            far_copy(h, 1).wait_recv()

        @pl.when(me >= 2 + 2 * core)
        def _():
            sib_copy(h, 1).start()

        @pl.when(h + 2 < KEY_VALUE_HEADS)
        def _():
            send_far(h + 2)

    def pass_on(h):
        part_copy(h).wait_recv()
        near = keep[h, 0] + theirs[h, 1 - core].astype(jnp.float32)
        out[h, 0] = near.astype(jnp.bfloat16)
        extra = jnp.where(core == 1, theirs[h, 1].astype(jnp.float32), 0.0)
        out[h, 1] = (keep[h, 1] + extra).astype(jnp.bfloat16)
        for i in (0, 1):

            @pl.when(me >= far[i])
            def _():
                out_copy(h, i).start()

    def store(h):
        cols = pl.ds(pl.multiple_of(h * width, width), width)
        return [
            pltpu.make_async_copy(o_ref.at[:, cols], o_hbm.at[:, cols], store_sem.at[h, 0]),
            pltpu.make_async_copy(dq_ref.at[:, cols], dq_hbm.at[:, cols], store_sem.at[h, 1]),
        ]

    def store_grads(h):
        cols = pl.ds(pl.multiple_of(h * HEAD_WIDTH, HEAD_WIDTH), HEAD_WIDTH)
        return [
            pltpu.make_async_copy(dk_ref.at[:, cols], dk_hbm.at[:, cols], store_sem.at[h, 2]),
            pltpu.make_async_copy(dv_ref.at[:, cols], dv_hbm.at[:, cols], store_sem.at[h, 3]),
        ]

    forward(0)
    load_q.wait()
    load_g.wait()

    def head(h, carry):
        for slot in (3, 1):

            @pl.when(me >= SPAN - slot)
            def _():
                sib_copy(h, slot).wait_recv()

        cols = pl.ds(pl.multiple_of(h * width, width), width)
        keys = win[h, 0].reshape(window, HEAD_WIDTH)
        values = win[h, 1].reshape(window, HEAD_WIDTH)
        q4 = stacked(q_ref[:, cols])
        g4 = stacked(g_ref[:, cols])
        scores = dot(keys, q4, 1, 1) + jnp.concatenate([bias[...]] * GROUP, axis=1)
        row_max = jnp.max(scores, axis=0, keepdims=True)
        weights = jnp.exp2((scores - row_max) * (scale / math.log(2.0)))
        inverse = 1.0 / jnp.sum(weights, axis=0, keepdims=True)
        mixed = dot(values, weights.astype(jnp.bfloat16), 0, 0) * inverse

        @pl.when(h + 1 < KEY_VALUE_HEADS)
        def _():
            forward(h + 1)

        @pl.when(h >= 1)
        def _():
            pass_on(h - 1)

        probs = weights * inverse
        prob_grads = dot(values, g4, 1, 1)
        terms = probs * prob_grads
        deltas = jnp.sum(terms, axis=0, keepdims=True)
        ds16 = (terms - probs * deltas).astype(jnp.bfloat16)
        p16 = probs.astype(jnp.bfloat16)
        dk = dot(ds16, q4, 1, 0) * scale
        dv = dot(p16, g4, 1, 0)
        for i, grad in enumerate((dk, dv)):
            blocks = [grad[b * rows : (b + 1) * rows] for b in range(SPAN + 1)]
            mine[h, 0, i] = blocks[3].astype(jnp.bfloat16)
            mine[h, 1, i] = blocks[1].astype(jnp.bfloat16)
            keep[h, 0, i] = blocks[2]
            keep[h, 1, i] = blocks[0]
            own[h, i] = blocks[4]
        part_copy(h).start()

        query_grad = dot(keys, ds16, 0, 0) * scale
        for j in range(GROUP):
            span = slice(j * rows, (j + 1) * rows)
            part = pl.ds(pl.multiple_of(h * width + j * HEAD_WIDTH, HEAD_WIDTH), HEAD_WIDTH)
            o_ref[:, part] = mixed[:, span].T.astype(jnp.bfloat16)
            dq_ref[:, part] = query_grad[:, span].T.astype(jnp.bfloat16)

        for copy in store(h):
            copy.start()
        return carry

    lax.fori_loop(0, KEY_VALUE_HEADS, head, 0)
    pass_on(KEY_VALUE_HEADS - 1)

    def finish(h, carry):
        for i in (0, 1):

            @pl.when(me + far[i] < count)
            def _():
                far_copy(h, i).wait_send()
                out_copy(h, i).wait_recv()

            @pl.when(me >= far[i])
            def _():
                out_copy(h, i).wait_send()

        @pl.when(me >= 2 * core)
        def _():
            sib_copy(h, 3).wait_send()

        @pl.when(me >= 2 + 2 * core)
        def _():
            sib_copy(h, 1).wait_send()

        part_copy(h).wait_send()
        total = own[h] + jnp.where(core == 0, theirs[h, 0].astype(jnp.float32), 0.0)
        for i in (0, 1):
            total = total + got[h, i].astype(jnp.float32)
        part = pl.ds(pl.multiple_of(h * HEAD_WIDTH, HEAD_WIDTH), HEAD_WIDTH)
        dk_ref[:, part] = total[0].astype(jnp.bfloat16)
        dv_ref[:, part] = total[1].astype(jnp.bfloat16)
        for copy in store_grads(h):
            copy.start()
        return carry

    lax.fori_loop(0, KEY_VALUE_HEADS, finish, 0)
    for h in range(KEY_VALUE_HEADS):
        for copy in store(h) + store_grads(h):
            copy.wait()


def place(*refs):
    sources, results, held, load_sem, store_sem = refs[:4], refs[4:8], refs[8:12], refs[12], refs[13]
    loads = [
        pltpu.make_async_copy(source, block, load_sem.at[i])
        for i, (source, block) in enumerate(zip(sources, held))
    ]
    stores = [
        pltpu.make_async_copy(block, result, store_sem.at[i])
        for i, (block, result) in enumerate(zip(held, results))
    ]
    for load in loads:
        load.start()
    for load, store in zip(loads, stores):
        load.wait()
        store.start()
    for store in stores:
        store.wait()


def solution(mesh):
    count = mesh.shape["dp"]

    def body(queries, key_vectors, value_vectors, output_gradient, doc_lengths):
        rows = queries.shape[0]
        hbm = pl.BlockSpec(memory_space=pl.ANY)
        pair = (2, rows, HEAD_WIDTH)
        heads = KEY_VALUE_HEADS
        arrays = (queries, queries, key_vectors, value_vectors)
        shapes = [jax.ShapeDtypeStruct(a.shape, jnp.bfloat16) for a in arrays]
        results = pl.pallas_call(
            functools.partial(kernel, count),
            out_shape=shapes,
            in_specs=[pl.BlockSpec(memory_space=pltpu.SMEM)] + [hbm] * 4,
            out_specs=[hbm] * 4,
            scratch_shapes=[pltpu.VMEM(a.shape, jnp.bfloat16) for a in arrays]
            + [
                pltpu.VMEM(queries.shape, jnp.bfloat16),
                pltpu.VMEM(queries.shape, jnp.bfloat16),
                pltpu.VMEM((heads, 2, SPAN + 1, rows, HEAD_WIDTH), jnp.bfloat16),
                pltpu.VMEM((heads, 2) + pair, jnp.bfloat16),
                pltpu.VMEM((heads, 2) + pair, jnp.bfloat16),
                pltpu.VMEM((heads, 2) + pair, jnp.float32),
                pltpu.VMEM((heads, 2) + pair, jnp.bfloat16),
                pltpu.VMEM((heads, 2) + pair, jnp.bfloat16),
                pltpu.VMEM((heads,) + pair, jnp.float32),
                pltpu.VMEM(((SPAN + 1) * rows, rows), jnp.float32),
                pltpu.SemaphoreType.DMA((2,)),
                pltpu.SemaphoreType.DMA((heads, 2)),
                pltpu.SemaphoreType.DMA((heads, 2)),
                pltpu.SemaphoreType.DMA((heads, 2)),
                pltpu.SemaphoreType.DMA((heads, SPAN)),
                pltpu.SemaphoreType.DMA((heads,)),
                pltpu.SemaphoreType.DMA((heads,)),
                pltpu.SemaphoreType.DMA((heads, 2)),
                pltpu.SemaphoreType.DMA((heads, 2)),
                pltpu.SemaphoreType.DMA((heads, 4)),
            ],
            compiler_params=pltpu.CompilerParams(
                collective_id=0, has_side_effects=True, vmem_limit_bytes=63 * 1024 * 1024
            ),
            cost_estimate=pl.CostEstimate(
                flops=10 * rows * rows * (SPAN + 1) * QUERY_HEADS * HEAD_WIDTH,
                bytes_accessed=12 * rows * QUERY_HEADS * HEAD_WIDTH,
                transcendentals=rows * rows * (SPAN + 1) * QUERY_HEADS,
            ),
        )(doc_lengths, queries, key_vectors, value_vectors, output_gradient)
        return pl.pallas_call(
            place,
            out_shape=shapes,
            in_specs=[hbm] * 4,
            out_specs=[hbm] * 4,
            scratch_shapes=[pltpu.VMEM(a.shape, jnp.bfloat16) for a in arrays]
            + [pltpu.SemaphoreType.DMA((4,))] * 2,
            compiler_params=pltpu.CompilerParams(vmem_limit_bytes=63 * 1024 * 1024),
        )(*results)

    spread = P(("groups", "dp"), None)
    return jax.shard_map(
        body,
        mesh=mesh,
        in_specs=(spread,) * 4 + (P("groups"),),
        out_specs=(spread,) * 4,
        check_vma=False,
    )
```
